128 devices in a mesh: row: 8 (over z, core), col: 16 (over y, x).
Axes of the slice: x: 4, y: 4, z: 4, core: 2. Of those that a mesh axis runs over, the one named last changes fastest.
Arguments:
- root_linv: float32 [4096, 4096], P('row', 'col'), as said below
- root_pivinv: float32 [4096], P('row'), may hold values from 0.25 to 4
- child_blocks: int32 [2, 8], replicated, may hold values from 0 to 15, as said below
- child_panel: float32 [2, 4096, 3072], P(None, 'col', 'row'), as said below
- child_base: float32 [2, 3072, 3072], P(None, 'col', 'row'), as said below
Outputs:
- root_inverse: float32 [4096, 4096], P('row', 'col')
- panel_inverse: float32 [2, 4096, 3072], P(None, 'col', 'row')
- diag_inverse: float32 [2, 3072, 3072], P(None, 'col', 'row')
The draws below stay inside these ranges and needn't reach their ends.
Inputs may be any that keep to these rules, and one draw needn't show every extreme that they name: `child_blocks`: each row lists 8 distinct block indices of the root in increasing order. child_panel[n] is zero on every root block row whose index child_blocks[n] does not list. `root_linv`: unit lower triangular. Each child_base[n] is symmetric.
All inputs are finite; a program needn't handle non-finite values.
Results may differ from the reference program's by a relative error of at most 0.000071.
Values sent between devices are 32-bit elements; how exact they have to be, the bound alone decides.
No kernel may reach another device: no remote copies, remote signals or barrier semaphores. Data moves between devices by JAX's collectives and lax.ppermute only.
A program may use at most 128 MiB of HBM per device.

```python
import math
import jax
import jax.numpy as jnp
from jax import lax

R = 4096
WC = 3072
BS = 256
NCH = 2
KB = 8


def block_lists(key):
    keys = jax.random.split(key, NCH)
    orders = jax.vmap(lambda sub: jax.random.permutation(sub, R // BS))(keys)
    return jnp.sort(orders[:, :KB], axis=1).astype(jnp.int32)


def draw_child_blocks(key, part):
    lists = block_lists(key)
    return lists


def draw_child_panel(key, part):
    lists = block_lists(key)
    key = jax.random.fold_in(key, 12)
    row_blocks = jnp.arange(R, dtype=jnp.int32) // BS
    inside = jnp.any(lists[:, :, None] == row_blocks[None, None, :], axis=1).astype(jnp.float32)
    values = jax.random.normal(key, (NCH, R, WC), jnp.float32)
    return values * inside[:, :, None] / math.sqrt(KB * BS)


def draw_root_linv(key, part):
    key = jax.random.fold_in(key, 13)
    values = jax.random.normal(key, (R, R), jnp.float32)
    lower = jnp.tril(values, -1) * (2.0 / math.sqrt(R))
    return lower + jnp.eye(R, dtype=jnp.float32)


def draw_child_base(key, part):
    key = jax.random.fold_in(key, 14)
    key_noise, key_pivots = jax.random.split(key)
    noise = jax.random.normal(key_noise, (NCH, WC, WC), jnp.float32)
    noise = noise * (0.5 / math.sqrt(WC))
    symmetric = noise + jnp.swapaxes(noise, 1, 2)
    pivots = jnp.exp(jax.random.uniform(key_pivots, (NCH, WC), jnp.float32, math.log(0.25), math.log(4.0)))
    return symmetric + pivots[:, :, None] * jnp.eye(WC, dtype=jnp.float32)[None, :, :]


def steps_of(rng, shape, pieces, low, largest):
    loudness = 1.0
    for axis_at, blocks in pieces:
        draws = jax.random.uniform(jax.random.fold_in(jax.random.fold_in(rng, 6), axis_at), (blocks,), jnp.float32, low / len(pieces), largest / len(pieces))
        loudness = loudness * jnp.repeat(jnp.exp(draws), shape[axis_at] // blocks).reshape((-1,) + (1,) * (len(shape) - 1 - axis_at))
    return loudness


def setup_inputs(seed: int = 0) -> dict:
    seeds = jax.random.split(jax.random.key(seed), 6)
    return {
        "root_linv": draw_root_linv(jax.random.fold_in(seeds[5], 71), 0),
        "root_pivinv": jnp.clip(jnp.exp(math.log(4.0) - 2.7725887 * jax.random.uniform(seeds[1], (R,), jnp.float32) ** steps_of(seeds[1], (R,), ((0, 8),), -0.2, 0.2)), 0.25, 4.0),
        "child_blocks": draw_child_blocks(jax.random.fold_in(seeds[5], 71), 0),
        "child_panel": draw_child_panel(jax.random.fold_in(seeds[5], 71), 0),
        "child_base": draw_child_base(jax.random.fold_in(seeds[5], 71), 0),
    }


def reference(root_linv, root_pivinv, child_blocks, child_panel, child_base):
    highest = lax.Precision.HIGHEST
    scaled = root_pivinv[:, None] * root_linv
    root_inverse = jnp.dot(root_linv.T, scaled, precision=highest, preferred_element_type=jnp.float32)
    row_blocks = jnp.arange(R, dtype=jnp.int32) // BS
    in_pattern = jnp.any(child_blocks[:, :, None] == row_blocks[None, None, :], axis=1).astype(jnp.float32)
    product = jnp.einsum("kj,nkw->njw", root_inverse, child_panel, precision=highest, preferred_element_type=jnp.float32)
    panel_inverse = -(in_pattern[:, :, None] * product)
    diag_inverse = child_base - jnp.einsum("njv,njw->nvw", child_panel, product, precision=highest, preferred_element_type=jnp.float32)
    return (root_inverse, panel_inverse, diag_inverse)
```

```python
import jax
import jax.numpy as jnp
from jax import lax
from jax.sharding import PartitionSpec as P

BS = 256
SIDE = 4
CORES = 2
AXES = ("row", "col")


def place(index):
    row, col = divmod(index, SIDE * SIDE)
    return col % SIDE, col // SIDE, row // CORES, row % CORES


def number(x, y, z, core):
    return ((z % SIDE) * CORES + core) * SIDE * SIDE + (y % SIDE) * SIDE + x % SIDE


def move(value, target):
    total = SIDE * SIDE * SIDE * CORES
    pairs = [(index, number(*target(*place(index)))) for index in range(total)]
    return lax.ppermute(value, AXES, pairs)


def shift(value, axis, step):
    if axis == "x":
        return move(value, lambda x, y, z, core: (x + step, y, z, core))
    if axis == "y":
        return move(value, lambda x, y, z, core: (x, y + step, z, core))
    return move(value, lambda x, y, z, core: (x, y, z + step, core))


def swap_cores(value):
    return move(value, lambda x, y, z, core: (x, y, z, 1 - core))


def gather(value, axis):
    return [value] + [shift(value, axis, -step) for step in range(1, SIDE)]


def scatter(pieces, axis):
    got = [shift(pieces[step], axis, step) for step in range(1, SIDE)]
    return pieces[0] + got[0] + got[1] + got[2]


def dot(left, right, contract):
    return lax.dot_general(
        left,
        right,
        ((contract[0], contract[1]), ((), ())),
        precision=lax.Precision.HIGH,
        preferred_element_type=jnp.float32,
    )


def tdot(left, right):
    return dot(left, right, ((0,), (0,)))


def take(value, at, size):
    return lax.dynamic_slice_in_dim(value, at * size, size, 0)


def shards(root_linv, root_pivinv, child_blocks, child_panel, child_base):
    row, col = lax.axis_index("row"), lax.axis_index("col")
    z, core = row // CORES, row % CORES
    y, x = col // SIDE, col % SIDE
    first, even = core == 0, x % 2 == 0
    panel0, panel1 = child_panel[0], child_panel[1]

    across = gather(root_linv, "x")
    down = jnp.concatenate(gather(root_pivinv[:, None] * root_linv, "y"), axis=1)
    low = jnp.concatenate(across[:2], axis=1)
    high = jnp.concatenate(across[2:], axis=1)
    got = swap_cores(tdot(down, jnp.where(first, high, low)))
    half = tdot(down, jnp.where(first, low, high)) + got
    piece = scatter([take(half, (z + step - y) % SIDE, BS) for step in range(SIDE)], "z")

    same = move(piece[:, :BS], lambda x, y, z, core: (x + 2 * core, y, z, x // 2))
    other = move(piece[:, BS:], lambda x, y, z, core: (x + 2 * core + 1, y, z, x // 2))
    root_inverse = jnp.concatenate([jnp.where(even, same, other), jnp.where(even, other, same)], axis=0)

    mine = jnp.concatenate(gather(piece, "z"), axis=0)
    theirs = swap_cores(mine)

    slab0 = jnp.concatenate(gather(panel0, "y"), axis=0)
    slab0 = lax.dynamic_slice_in_dim(
        jnp.concatenate([slab0, slab0], axis=0), ((z - y) % SIDE) * BS, SIDE * BS, 0
    )
    slab1 = gather(panel1, "x")
    low1 = jnp.concatenate(slab1[:2], axis=0)
    high1 = jnp.concatenate(slab1[2:], axis=0)

    part0_mine, part0_theirs = tdot(mine, slab0), tdot(theirs, slab0)
    part0 = jnp.concatenate(
        [jnp.where(first, part0_mine, part0_theirs), jnp.where(first, part0_theirs, part0_mine)], axis=0
    )
    part1 = dot(mine, jnp.where(first, low1, high1), ((1,), (0,))) + dot(
        theirs, jnp.where(first, high1, low1), ((1,), (0,))
    )
    product0 = scatter([part0[step * BS : (step + 1) * BS] for step in range(SIDE)], "x")
    product1 = scatter([take(part1, (step + y - z) % SIDE, BS) for step in range(SIDE)], "y")
    in_pattern = jnp.any(child_blocks == col, axis=1).astype(jnp.float32)
    panel_inverse = jnp.stack([-(in_pattern[0] * product0), -(in_pattern[1] * product1)])

    planes = gather(child_panel, "z")
    width = child_base.shape[1]
    left0 = jnp.concatenate([plane[0][:, :width] for plane in planes], axis=1)
    right0 = jnp.concatenate([plane[0][:, width:] for plane in planes], axis=1)
    alike = move(jnp.where(even, left0, right0), lambda x, y, z, core: (2 * core + x % 2, y, z, x // 2))
    unlike = move(jnp.where(even, right0, left0), lambda x, y, z, core: (2 * core + 1 - x % 2, y, z, x // 2))
    held = jnp.concatenate([jnp.where(even, alike, unlike), jnp.where(even, unlike, alike)], axis=0)
    handed = swap_cores(held)
    held_low, held_high = jnp.where(first, held, handed), jnp.where(first, handed, held)
    columns0 = lax.dynamic_slice_in_dim(
        jnp.concatenate([held_low, held_high, held_low, held_high], axis=0), x * BS, SIDE * BS, 0
    )
    stacked = jnp.concatenate([plane[1] for plane in planes], axis=0)
    kept = [take(stacked, (y + step - z) % SIDE, BS) for step in range(SIDE)]
    own1 = jnp.concatenate([kept[0]] + [shift(kept[SIDE - step], "y", -step) for step in range(1, SIDE)], axis=0)
    its1 = swap_cores(own1)
    columns1 = jnp.concatenate([jnp.where(first, own1, its1), jnp.where(first, its1, own1)], axis=1)

    diag0 = tdot(columns0, jnp.concatenate(gather(product0, "x"), axis=0))
    diag1 = tdot(columns1, jnp.concatenate(gather(product1, "y"), axis=0))
    sum0 = scatter([take(diag0, (step + y - z) % SIDE, width) for step in range(SIDE)], "y")
    sum1 = scatter([take(diag1, (step + x) % SIDE, width) for step in range(SIDE)], "x")
    diag_inverse = jnp.stack([child_base[0] - sum0, child_base[1] - sum1])
    return root_inverse, panel_inverse, diag_inverse


def solution(mesh):
    return jax.shard_map(
        shards,
        mesh=mesh,
        in_specs=(P("row", "col"), P("row"), P(), P(None, "col", "row"), P(None, "col", "row")),
        out_specs=(P("row", "col"), P(None, "col", "row"), P(None, "col", "row")),
        check_vma=False,
    )
```

```python
import jax
import jax.numpy as jnp
from jax import lax
from jax.sharding import PartitionSpec as P

BS = 256
SIDE = 4
CORES = 2
AXES = ("row", "col")


def place(index):
    row, col = divmod(index, SIDE * SIDE)
    return col % SIDE, col // SIDE, row // CORES, row % CORES


def number(x, y, z, core):
    return ((z % SIDE) * CORES + core) * SIDE * SIDE + (y % SIDE) * SIDE + x % SIDE


def move(value, target):
    total = SIDE * SIDE * SIDE * CORES
    pairs = [(index, number(*target(*place(index)))) for index in range(total)]
    return lax.ppermute(value, AXES, pairs)


def shift(value, axis, step):
    def target(x, y, z, core):
        if axis == "z":
            return x, y, z + step, core
        if axis == "x" or (axis == "along" and core == 0) or (axis == "across" and core == 1):
            return x + step, y, z, core
        return x, y + step, z, core

    return move(value, target)


def swap_cores(value):
    return move(value, lambda x, y, z, core: (x, y, z, 1 - core))


def gather(value, axis):
    return [value] + [shift(value, axis, -step) for step in (1, 2, 3)]


def scatter(pieces, axis):
    got = [shift(pieces[step], axis, step) for step in (2, 1, 3)]
    return pieces[0] + got[0] + got[1] + got[2]


def gather_halves(value, axis):
    half = value.shape[0] // 2
    below, above = shift(value, axis, 1), shift(value, axis, -1)
    top, bottom = shift(below[:half], axis, 1), shift(above[half:], axis, -1)
    return [value, above, jnp.concatenate([top, bottom], axis=0), below]


def gather_groups(value):
    groups = [[number(x, y, z, 0) for y in range(SIDE)] for z in range(SIDE) for x in range(SIDE)]
    groups += [[number(x, y, z, 1) for x in range(SIDE)] for z in range(SIDE) for y in range(SIDE)]
    return lax.all_gather(value, AXES, axis_index_groups=groups, axis=0, tiled=True)


def after(value, *earlier):
    return lax.optimization_barrier((value,) + earlier)[0]


def named(name, call, *args):
    with jax.named_scope(name):
        return call(*args)


def dot(left, right, dims):
    return lax.dot_general(
        left,
        right,
        (dims, ((), ())),
        precision=lax.Precision.HIGH,
        preferred_element_type=jnp.float32,
    )


def tdot(left, right):
    return dot(left, right, ((0,), (0,)))


def ndot(left, right):
    return dot(left, right, ((1,), (0,)))


def take(value, at, size):
    return lax.dynamic_slice_in_dim(value, at * size, size, 0)


def shards(root_linv, root_pivinv, child_blocks, child_panel, child_base):
    row, col = lax.axis_index("row"), lax.axis_index("col")
    z, core = row // CORES, row % CORES
    y, x = col // SIDE, col % SIDE
    first, even = core == 0, x % 2 == 0
    steps = range(SIDE)
    wide = child_panel.shape[2]
    width = child_base.shape[1]

    def pick(ours, theirs):
        return jnp.where(first, ours, theirs)

    got = named("panel_swap", swap_cores, pick(child_panel[1], child_panel[0]))
    kept = pick(child_panel[0], child_panel[1])
    panel = jnp.concatenate([pick(kept, got), pick(got, kept)], axis=1)

    scaled = root_pivinv[:, None] * root_linv
    own, got = pick(root_linv, scaled), named("root_swap", swap_cores, pick(scaled, root_linv))
    rows = jnp.concatenate([pick(own, got), pick(got, own)], axis=0)
    rows = named("root_rows", gather_halves, rows, "along")
    handed = [named("root_hand", swap_cores, value) for value in rows]
    tall = jnp.concatenate([pick(handed[step], rows[step]) for step in steps], axis=1)
    across = jnp.concatenate([pick(rows[step], handed[step + 2]) for step in (0, 1)], axis=1)

    half = tdot(tall, across)

    planes = lax.all_gather(child_panel, "row", axis=2, tiled=True)

    def columns(step):
        at = (x + step) % SIDE * width
        strips = [
            lax.dynamic_slice_in_dim(planes[0, :, n * SIDE * width : (n + 1) * SIDE * width], at, width, 1)
            for n in range(SIDE)
        ]
        whole = lax.dynamic_slice_in_dim(planes[1], ((y + step) % SIDE) * SIDE * width, SIDE * width, 1)
        return pick(jnp.concatenate(strips, axis=1), whole)

    strips = [columns(step) for step in steps]

    with jax.named_scope("piece_sum"):
        pieces = [take(half, (z + step - y) % SIDE, BS) for step in steps]
        received = [shift(pieces[step], "z", step) for step in (2, 1, 3)]
        received, strips = after((received, strips))
        piece = pieces[0] + received[0] + received[1] + received[2]

    mine = named("block_gather", gather, piece, "z")
    with jax.named_scope("block_swap"):
        theirs = jnp.concatenate([swap_cores(value) for value in mine], axis=0)
    mine = jnp.concatenate(mine, axis=0)

    with jax.named_scope("panel_columns"):
        left = [shift(strips[3], "along", -1), shift(strips[1], "along", 1)]
        far = shift(after(strips[2], *left), "along", 2)
        left = jnp.concatenate([strips[0], left[0], far, left[1]], axis=0)

    slab = named("panel_rows", gather_groups, panel)
    slab = jnp.concatenate([take(slab, (pick(z, x) + step) % SIDE, BS) for step in steps], axis=0)

    turn = after(piece, mine)
    same = named("root_same", move, turn[:, :BS], lambda x, y, z, core: (x + 2 * core, y, z, x // 2))
    other = named("root_other", move, turn[:, BS:], lambda x, y, z, core: (x + 2 * core + 1, y, z, x // 2))
    root_inverse = jnp.concatenate([pick_even(even, same, other), pick_even(even, other, same)], axis=0)
    mine = after(mine, far)

    def product_of_first(mine, theirs, slab):
        return jnp.concatenate([tdot(mine, slab), tdot(theirs, slab)], axis=0)

    def product_of_second(mine, theirs, slab):
        return ndot(mine, slab[2 * BS :]) + ndot(theirs, slab[: 2 * BS])

    part = lax.cond(first, product_of_first, product_of_second, mine, theirs, slab)
    part = after(part, same, other)
    part = [take(part, pick(step, (y + step - z) % SIDE), BS) for step in steps]
    product = named("product_sum", scatter, part, "along")

    diag = tdot(left, jnp.concatenate(named("product_rows", gather, product, "along"), axis=0))
    diag = [take(diag, pick((y + step) % SIDE, (x + step) % SIDE), width) for step in steps]
    diag = named("diag_sum", scatter, diag, "across")

    def placed(value):
        low, high = value[:, :wide], value[:, wide:]
        kept, got = pick(low, high), swap_cores(pick(high, low))
        return pick(kept, got), pick(got, kept)

    in_pattern = jnp.any(child_blocks == col, axis=1).astype(jnp.float32)
    panels = named("product_swap", placed, product)
    panel_inverse = jnp.stack([-(in_pattern[n] * panels[n]) for n in range(CORES)])
    diags = named("diag_swap", placed, diag)
    diag_inverse = jnp.stack([child_base[n] - diags[n] for n in range(CORES)])
    return root_inverse, panel_inverse, diag_inverse


def pick_even(even, ours, theirs):
    return jnp.where(even, ours, theirs)


def solution(mesh):
    return jax.shard_map(
        shards,
        mesh=mesh,
        in_specs=(P("row", "col"), P("row"), P(), P(None, "col", "row"), P(None, "col", "row")),
        out_specs=(P("row", "col"), P(None, "col", "row"), P(None, "col", "row")),
        check_vma=False,
    )
```

```python
import jax
import jax.numpy as jnp
from jax import lax
from jax.sharding import PartitionSpec as P

BS = 256
SIDE = 4
CORES = 2
AXES = ("row", "col")


def place(index):
    row, col = divmod(index, SIDE * SIDE)
    return col % SIDE, col // SIDE, row // CORES, row % CORES


def number(x, y, z, core):
    return ((z % SIDE) * CORES + core) * SIDE * SIDE + (y % SIDE) * SIDE + x % SIDE


def move(value, target):
    total = SIDE * SIDE * SIDE * CORES
    pairs = [(index, number(*target(*place(index)))) for index in range(total)]
    return lax.ppermute(value, AXES, pairs)


def shift(value, axis, step):
    def target(x, y, z, core):
        if axis == "z":
            return x, y, z + step, core
        if axis == "x" or (axis == "along" and core == 0) or (axis == "across" and core == 1):
            return x + step, y, z, core
        return x, y + step, z, core

    return move(value, target)


def swap_cores(value):
    return move(value, lambda x, y, z, core: (x, y, z, 1 - core))


def gather(value, axis):
    return [value] + [shift(value, axis, -step) for step in (1, 2, 3)]


def scatter(pieces, axis):
    got = [shift(pieces[step], axis, step) for step in (1, 2, 3)]
    return pieces[0] + got[0] + got[1] + got[2]


def sides(value, axis):
    return shift(value, axis, -1), shift(value, axis, 1)


def gather_groups(value):
    groups = [[number(x, y, z, 0) for y in range(SIDE)] for z in range(SIDE) for x in range(SIDE)]
    groups += [[number(x, y, z, 1) for x in range(SIDE)] for z in range(SIDE) for y in range(SIDE)]
    return lax.all_gather(value, AXES, axis_index_groups=groups, axis=0, tiled=True)


def after(value, *earlier):
    return lax.optimization_barrier((value,) + earlier)[0]


def named(name, call, *args):
    with jax.named_scope(name):
        return call(*args)


def dot(left, right, dims):
    return lax.dot_general(
        left,
        right,
        (dims, ((), ())),
        precision=lax.Precision.HIGH,
        preferred_element_type=jnp.float32,
    )


def tdot(left, right):
    return dot(left, right, ((0,), (0,)))


def ndot(left, right):
    return dot(left, right, ((1,), (0,)))


def take(value, at, size):
    return lax.dynamic_slice_in_dim(value, at * size, size, 0)


def shards(root_linv, root_pivinv, child_blocks, child_panel, child_base):
    row, col = lax.axis_index("row"), lax.axis_index("col")
    z, core = row // CORES, row % CORES
    y, x = col // SIDE, col % SIDE
    first, even = core == 0, x % 2 == 0
    steps = range(SIDE)
    wide = child_panel.shape[2]
    width = child_base.shape[1]

    def pick(ours, theirs):
        return jnp.where(first, ours, theirs)

    with jax.named_scope("root_rows"):
        above, below = sides(root_linv, "along")
        other = swap_cores(root_linv)
        above_other, below_other = sides(other, "along")
        far, far_other = shift(below, "along", 1), shift(above_other, "along", -1)
    rows = [root_linv, above, far, below], [other, above_other, far_other, below_other]

    children = after(child_panel, other)
    got = named("panel_swap", swap_cores, pick(children[1], children[0]))
    kept = pick(children[0], children[1])
    panel = jnp.concatenate([pick(kept, got), pick(got, kept)], axis=1)

    with jax.named_scope("root_hand"):
        handed = [[kept[0]] + [swap_cores(value) for value in sent[1:]] for kept, sent in zip(rows, rows[::-1])]
        scales = root_pivinv, swap_cores(root_pivinv)

    terms = []
    for scale, kept, got in zip(scales, rows, handed):
        tall = jnp.concatenate([pick(got[step], kept[step]) for step in steps], axis=1)
        across = jnp.concatenate([pick(kept[step], got[step + 2]) for step in (0, 1)], axis=1)
        terms.append(tdot(scale[:, None] * tall, across))
    half = terms[0] + terms[1]

    planes = lax.all_gather(child_panel, "row", axis=2, tiled=True)

    def columns(step):
        at = (x + step) % SIDE * width
        strips = [
            lax.dynamic_slice_in_dim(planes[0, :, n * SIDE * width : (n + 1) * SIDE * width], at, width, 1)
            for n in range(SIDE)
        ]
        whole = lax.dynamic_slice_in_dim(planes[1], ((y + step) % SIDE) * SIDE * width, SIDE * width, 1)
        return pick(jnp.concatenate(strips, axis=1), whole)

    strips = [columns(step) for step in steps]

    with jax.named_scope("piece_sum"):
        pieces = [take(half, (z + step - y) % SIDE, BS) for step in steps]
        received = [shift(pieces[step], "z", step) for step in (1, 2, 3)]
        received, strips = after((received, strips))
        piece = pieces[0] + received[0] + received[1] + received[2]

    mine = named("block_gather", gather, piece, "z")
    with jax.named_scope("block_swap"):
        theirs = jnp.concatenate([swap_cores(value) for value in mine], axis=0)
    mine = jnp.concatenate(mine, axis=0)

    with jax.named_scope("panel_columns"):
        left = [shift(strips[3], "along", -1), shift(strips[1], "along", 1)]
        far = shift(after(strips[2], *left), "along", 2)
        left = jnp.concatenate([strips[0], left[0], far, left[1]], axis=0)

    slab = named("panel_rows", gather_groups, panel)
    slab = jnp.concatenate([take(slab, (pick(z, x) + step) % SIDE, BS) for step in steps], axis=0)

    def product_of_first(mine, theirs, slab):
        return jnp.concatenate([tdot(mine, slab), tdot(theirs, slab)], axis=0)

    def product_of_second(mine, theirs, slab):
        return ndot(mine, slab[2 * BS :]) + ndot(theirs, slab[: 2 * BS])

    part = lax.cond(first, product_of_first, product_of_second, mine, theirs, slab)
    part = after(part, far)
    part = [take(part, pick(step, (y + step - z) % SIDE), BS) for step in steps]
    product = named("product_sum", scatter, part, "along")

    turn = after(piece, product)
    same = named("root_same", move, turn[:, :BS], lambda x, y, z, core: (x + 2 * core, y, z, x // 2))
    other = named("root_other", move, turn[:, BS:], lambda x, y, z, core: (x + 2 * core + 1, y, z, x // 2))

    gathered = named("product_rows", gather, product, "along")
    gathered, same, other = after((gathered, same, other))
    diag = tdot(left, jnp.concatenate(gathered, axis=0))
    diag = [take(diag, pick((y + step) % SIDE, (x + step) % SIDE), width) for step in steps]
    diag = named("diag_sum", scatter, diag, "across")

    root_inverse = jnp.concatenate([pick_even(even, same, other), pick_even(even, other, same)], axis=0)

    def placed(value):
        low, high = value[:, :wide], value[:, wide:]
        kept, got = pick(low, high), swap_cores(pick(high, low))
        return pick(kept, got), pick(got, kept)

    in_pattern = jnp.any(child_blocks == col, axis=1).astype(jnp.float32)
    panels = named("product_swap", placed, product)
    panel_inverse = jnp.stack([-(in_pattern[n] * panels[n]) for n in range(CORES)])
    diags = named("diag_swap", placed, diag)
    diag_inverse = jnp.stack([child_base[n] - diags[n] for n in range(CORES)])
    return root_inverse, panel_inverse, diag_inverse


def pick_even(even, ours, theirs):
    return jnp.where(even, ours, theirs)


def solution(mesh):
    return jax.shard_map(
        shards,
        mesh=mesh,
        in_specs=(P("row", "col"), P("row"), P(), P(None, "col", "row"), P(None, "col", "row")),
        out_specs=(P("row", "col"), P(None, "col", "row"), P(None, "col", "row")),
        check_vma=False,
    )
```

```python
import jax
import jax.numpy as jnp
from jax import lax
from jax.sharding import PartitionSpec as P

BS = 256
SIDE = 4
CORES = 2
AXES = ("row", "col")


def place(index):
    row, col = divmod(index, SIDE * SIDE)
    return col % SIDE, col // SIDE, row // CORES, row % CORES


def number(x, y, z, core):
    return ((z % SIDE) * CORES + core) * SIDE * SIDE + (y % SIDE) * SIDE + x % SIDE


def move(value, target):
    total = SIDE * SIDE * SIDE * CORES
    pairs = [(index, number(*target(*place(index)))) for index in range(total)]
    return lax.ppermute(value, AXES, pairs)


def shift(value, axis, step):
    def target(x, y, z, core):
        if axis == "z":
            return x, y, z + step, core
        if axis == "x" or (axis == "along" and core == 0) or (axis == "across" and core == 1):
            return x + step, y, z, core
        return x, y + step, z, core

    return move(value, target)


def swap_cores(value):
    return move(value, lambda x, y, z, core: (x, y, z, 1 - core))


def gather(value, axis):
    return [value] + [shift(value, axis, -step) for step in (1, 2, 3)]


def scatter(pieces, axis):
    got = [shift(pieces[step], axis, step) for step in (1, 2, 3)]
    return pieces[0] + got[0] + got[1] + got[2]


def sides(value, axis):
    return shift(value, axis, -1), shift(value, axis, 1)


def opposite(above, below, axis):
    half = above.shape[0] // 2
    top, bottom = shift(below[:half], axis, 1), shift(above[half:], axis, -1)
    return jnp.concatenate([top, bottom], axis=0)


def relay(value):
    return move(value, lambda x, y, z, core: (x, y, z + 1 - 2 * core, core))


def after(value, *earlier):
    return lax.optimization_barrier((value,) + earlier)[0]


def named(name, call, *args):
    with jax.named_scope(name):
        return call(*args)


def dot(left, right, dims):
    return lax.dot_general(
        left,
        right,
        (dims, ((), ())),
        precision=lax.Precision.HIGH,
        preferred_element_type=jnp.float32,
    )


def tdot(left, right):
    return dot(left, right, ((0,), (0,)))


def ndot(left, right):
    return dot(left, right, ((1,), (0,)))


def take(value, at, size):
    return lax.dynamic_slice_in_dim(value, at * size, size, 0)


def shards(root_linv, root_pivinv, child_blocks, child_panel, child_base):
    row, col = lax.axis_index("row"), lax.axis_index("col")
    z, core = row // CORES, row % CORES
    y, x = col // SIDE, col % SIDE
    first, even = core == 0, x % 2 == 0
    steps = range(SIDE)
    wide = child_panel.shape[2]
    width = child_base.shape[1]

    def pick(ours, theirs):
        return jnp.where(first, ours, theirs)

    with jax.named_scope("root_rows"):
        above, below = sides(root_linv, "along")
        other = swap_cores(root_linv)
        above_other, below_other = sides(other, "along")
    with jax.named_scope("panel_planes"):
        lent = swap_cores(child_panel)
        near = relay(child_panel)
        passed = relay(lent)
        above_other, near, passed = after((above_other, near, passed))
        beyond = relay(near)
    with jax.named_scope("root_rows"):
        far, far_other = shift(below, "along", 1), shift(above_other, "along", -1)
    rows = [root_linv, above, far, below], [other, above_other, far_other, below_other]

    with jax.named_scope("root_hand"):
        handed = [[kept[0]] + [swap_cores(value) for value in sent[1:]] for kept, sent in zip(rows, rows[::-1])]
        scales = root_pivinv, swap_cores(root_pivinv)

    terms = []
    for scale, kept, got in zip(scales, rows, handed):
        tall = jnp.concatenate([pick(got[step], kept[step]) for step in steps], axis=1)
        across = jnp.concatenate([pick(kept[step], got[step + 2]) for step in (0, 1)], axis=1)
        terms.append(tdot(scale[:, None] * tall, across))
    half = terms[0] + terms[1]

    def joined(low, high):
        return jnp.concatenate([low, high], axis=1)

    panel = joined(pick(child_panel[0], lent[1]), pick(lent[0], child_panel[1]))
    near_plane = joined(pick(near[0], passed[1]), pick(passed[0], near[1]))
    opposite_plane = joined(pick(near[1], passed[0]), pick(passed[1], near[0]))
    opposite_plane = named("panel_hand", swap_cores, opposite_plane)
    above_plane, below_plane = pick(opposite_plane, near_plane), pick(near_plane, opposite_plane)
    half, beyond, panel, above_plane, below_plane = after((half, beyond, panel, above_plane, below_plane))

    above, below = named("panel_rows", sides, panel, "across")
    slab = [panel, above, named("panel_rows", opposite, above, below, "across"), below]

    got = named("panel_hand", swap_cores, pick(beyond[1], beyond[0]))
    planes = [panel, above_plane, joined(pick(beyond[0], got), pick(got, beyond[1])), below_plane]
    stacked = jnp.concatenate(planes, axis=0)

    def columns(step):
        at = (x + step) % SIDE * width
        strips = [lax.dynamic_slice_in_dim(plane, at, width, 1) for plane in planes]
        return pick(jnp.concatenate(strips, axis=1), take(stacked, (y + step - z) % SIDE, BS))

    strips = [columns(step) for step in steps]

    with jax.named_scope("piece_sum"):
        pieces = [take(half, (z + step - y) % SIDE, BS) for step in steps]
        received = [shift(pieces[step], "z", step) for step in (1, 2, 3)]
        received, slab, strips = after((received, slab, strips))
        piece = pieces[0] + received[0] + received[1] + received[2]

    mine = named("block_gather", gather, piece, "z")
    with jax.named_scope("block_swap"):
        theirs = jnp.concatenate([swap_cores(value) for value in mine], axis=0)
    mine = jnp.concatenate(mine, axis=0)

    with jax.named_scope("panel_columns"):
        left = [shift(strips[3], "along", -1), shift(strips[1], "along", 1)]
        far = shift(after(strips[2], *left), "along", 2)
        left = jnp.concatenate([strips[0], left[0], far, left[1]], axis=0)

    slab = jnp.concatenate(slab, axis=0)
    slab = jnp.concatenate([take(slab, pick((z + step - y) % SIDE, step), BS) for step in steps], axis=0)

    def product_of_first(mine, theirs, slab):
        return jnp.concatenate([tdot(mine, slab), tdot(theirs, slab)], axis=0)

    def product_of_second(mine, theirs, slab):
        return ndot(mine, slab[2 * BS :]) + ndot(theirs, slab[: 2 * BS])

    part = lax.cond(first, product_of_first, product_of_second, mine, theirs, slab)
    part = after(part, far)
    part = [take(part, pick(step, (y + step - z) % SIDE), BS) for step in steps]
    product = named("product_sum", scatter, part, "along")

    turn = after(piece, product)
    same = named("root_same", move, turn[:, :BS], lambda x, y, z, core: (x + 2 * core, y, z, x // 2))
    other = named("root_other", move, turn[:, BS:], lambda x, y, z, core: (x + 2 * core + 1, y, z, x // 2))

    gathered = named("product_rows", gather, product, "along")
    gathered, same, other = after((gathered, same, other))
    diag = tdot(left, jnp.concatenate(gathered, axis=0))
    diag = [take(diag, pick((y + step - z) % SIDE, (x + step) % SIDE), width) for step in steps]
    diag = named("diag_sum", scatter, diag, "across")

    root_inverse = jnp.concatenate([pick_even(even, same, other), pick_even(even, other, same)], axis=0)

    def placed(value):
        low, high = value[:, :wide], value[:, wide:]
        kept, got = pick(low, high), swap_cores(pick(high, low))
        return pick(kept, got), pick(got, kept)

    in_pattern = jnp.any(child_blocks == col, axis=1).astype(jnp.float32)
    panels = named("product_swap", placed, product)
    panel_inverse = jnp.stack([-(in_pattern[n] * panels[n]) for n in range(CORES)])
    diags = named("diag_swap", placed, diag)
    diag_inverse = jnp.stack([child_base[n] - diags[n] for n in range(CORES)])
    return root_inverse, panel_inverse, diag_inverse


def pick_even(even, ours, theirs):
    return jnp.where(even, ours, theirs)


def solution(mesh):
    return jax.shard_map(
        shards,
        mesh=mesh,
        in_specs=(P("row", "col"), P("row"), P(), P(None, "col", "row"), P(None, "col", "row")),
        out_specs=(P("row", "col"), P(None, "col", "row"), P(None, "col", "row")),
        check_vma=False,
    )
```

```python
import jax
import jax.numpy as jnp
from jax import lax
from jax.sharding import PartitionSpec as P

BS = 256
SIDE = 4
CORES = 2
AXES = ("row", "col")


def place(index):
    row, col = divmod(index, SIDE * SIDE)
    return col % SIDE, col // SIDE, row // CORES, row % CORES


def number(x, y, z, core):
    return ((z % SIDE) * CORES + core) * SIDE * SIDE + (y % SIDE) * SIDE + x % SIDE


def move(value, target):
    total = SIDE * SIDE * SIDE * CORES
    pairs = [(index, number(*target(*place(index)))) for index in range(total)]
    return lax.ppermute(value, AXES, pairs)


def shift(value, axis, step):
    def target(x, y, z, core):
        if axis == "z":
            return x, y, z + step, core
        if axis == "x" or (axis == "along" and core == 0) or (axis == "across" and core == 1):
            return x + step, y, z, core
        return x, y + step, z, core

    return move(value, target)


def swap_cores(value):
    return move(value, lambda x, y, z, core: (x, y, z, 1 - core))


def gather(value, axis):
    return [value] + [shift(value, axis, -step) for step in (1, 2, 3)]


def scatter(pieces, axis):
    got = [shift(pieces[step], axis, step) for step in (1, 2, 3)]
    return pieces[0] + got[0] + got[1] + got[2]


def sides(value, axis):
    return shift(value, axis, -1), shift(value, axis, 1)


def opposite(above, below, axis):
    half = above.shape[0] // 2
    top, bottom = shift(below[:half], axis, 1), shift(above[half:], axis, -1)
    return jnp.concatenate([top, bottom], axis=0)


def relay(value):
    return move(value, lambda x, y, z, core: (x, y, z + 1 - 2 * core, core))


def after(value, *earlier):
    return lax.optimization_barrier((value,) + earlier)[0]


def named(name, call, *args):
    with jax.named_scope(name):
        return call(*args)


def dot(left, right, dims):
    return lax.dot_general(
        left,
        right,
        (dims, ((), ())),
        precision=lax.Precision.HIGH,
        preferred_element_type=jnp.float32,
    )


def tdot(left, right):
    return dot(left, right, ((0,), (0,)))


def ndot(left, right):
    return dot(left, right, ((1,), (0,)))


def take(value, at, size):
    return lax.dynamic_slice_in_dim(value, at * size, size, 0)


def shards(root_linv, root_pivinv, child_blocks, child_panel, child_base):
    row, col = lax.axis_index("row"), lax.axis_index("col")
    z, core = row // CORES, row % CORES
    y, x = col // SIDE, col % SIDE
    first, even = core == 0, x % 2 == 0
    steps = range(SIDE)
    wide = child_panel.shape[2]
    width = child_base.shape[1]

    def pick(ours, theirs):
        return jnp.where(first, ours, theirs)

    with jax.named_scope("root_rows"):
        above, below = sides(root_linv, "along")
        other = swap_cores(root_linv)
        above_other, below_other = sides(other, "along")
    with jax.named_scope("panel_planes"):
        lent = swap_cores(child_panel)
        near = relay(child_panel)
        passed = relay(after(lent, near, above_other))
    with jax.named_scope("root_rows"):
        far, far_other = shift(below, "along", 1), shift(above_other, "along", -1)
    with jax.named_scope("panel_planes"):
        far_other, passed = after((far_other, passed))
        beyond = relay(after(near, passed))
    rows = [root_linv, above, far, below], [other, above_other, far_other, below_other]

    with jax.named_scope("root_hand"):
        handed = [[kept[0]] + [swap_cores(value) for value in sent[1:]] for kept, sent in zip(rows, rows[::-1])]
        scales = root_pivinv, swap_cores(root_pivinv)

    terms = []
    for scale, kept, got in zip(scales, rows, handed):
        tall = jnp.concatenate([pick(got[step], kept[step]) for step in steps], axis=1)
        across = jnp.concatenate([pick(kept[step], got[step + 2]) for step in (0, 1)], axis=1)
        terms.append(tdot(scale[:, None] * tall, across))
    half = terms[0] + terms[1]

    def joined(low, high):
        return jnp.concatenate([low, high], axis=1)

    panel = joined(pick(child_panel[0], lent[1]), pick(lent[0], child_panel[1]))
    near_plane = joined(pick(near[0], passed[1]), pick(passed[0], near[1]))
    opposite_plane = joined(pick(near[1], passed[0]), pick(passed[1], near[0]))
    opposite_plane = named("panel_hand", swap_cores, opposite_plane)
    above_plane, below_plane = pick(opposite_plane, near_plane), pick(near_plane, opposite_plane)
    above, below = named("panel_rows", sides, panel, "across")
    held = half, panel, above_plane, below_plane, above, below
    half, panel, above_plane, below_plane, above, below = after(held)

    got = named("panel_hand", swap_cores, pick(beyond[1], beyond[0]))
    above, below, got = after((above, below, got))
    slab = [panel, above, named("panel_rows", opposite, above, below, "across"), below]
    planes = [panel, above_plane, joined(pick(beyond[0], got), pick(got, beyond[1])), below_plane]
    stacked = jnp.concatenate(planes, axis=0)

    def columns(step):
        at = (x + step) % SIDE * width
        strips = [lax.dynamic_slice_in_dim(plane, at, width, 1) for plane in planes]
        return pick(jnp.concatenate(strips, axis=1), take(stacked, (y + step - z) % SIDE, BS))

    strips = [columns(step) for step in steps]

    with jax.named_scope("piece_sum"):
        pieces = [take(half, (z + step - y) % SIDE, BS) for step in steps]
        received = [shift(pieces[step], "z", step) for step in (1, 2, 3)]
        received, slab, strips = after((received, slab, strips))
        piece = pieces[0] + received[0] + received[1] + received[2]

    mine = named("block_gather", gather, piece, "z")
    with jax.named_scope("block_swap"):
        theirs = jnp.concatenate([swap_cores(value) for value in mine], axis=0)
    mine = jnp.concatenate(mine, axis=0)

    with jax.named_scope("panel_columns"):
        left = [shift(strips[3], "along", -1), shift(strips[1], "along", 1)]
        far = shift(after(strips[2], *left), "along", 2)
        left = jnp.concatenate([strips[0], left[0], far, left[1]], axis=0)

    slab = jnp.concatenate(slab, axis=0)
    slab = jnp.concatenate([take(slab, pick((z + step - y) % SIDE, step), BS) for step in steps], axis=0)

    def product_of_first(mine, theirs, slab):
        return jnp.concatenate([tdot(mine, slab), tdot(theirs, slab)], axis=0)

    def product_of_second(mine, theirs, slab):
        return ndot(mine, slab[2 * BS :]) + ndot(theirs, slab[: 2 * BS])

    part = lax.cond(first, product_of_first, product_of_second, mine, theirs, slab)
    part = after(part, far)
    part = [take(part, pick(step, (y + step - z) % SIDE), BS) for step in steps]
    product = named("product_sum", scatter, part, "along")

    gathered = named("product_rows", gather, product, "along")
    diag = tdot(left, jnp.concatenate(gathered, axis=0))

    turn = after(piece, diag)
    same = named("root_same", move, turn[:, :BS], lambda x, y, z, core: (x + 2 * core, y, z, x // 2))
    other = named("root_other", move, turn[:, BS:], lambda x, y, z, core: (x + 2 * core + 1, y, z, x // 2))

    diag = [take(diag, pick((y + step - z) % SIDE, (x + step) % SIDE), width) for step in steps]
    diag = named("diag_sum", scatter, diag, "across")
    diag, same, other = after((diag, same, other))

    root_inverse = jnp.concatenate([pick_even(even, same, other), pick_even(even, other, same)], axis=0)

    def placed(value):
        low, high = value[:, :wide], value[:, wide:]
        kept, got = pick(low, high), swap_cores(pick(high, low))
        return pick(kept, got), pick(got, kept)

    in_pattern = jnp.any(child_blocks == col, axis=1).astype(jnp.float32)
    panels = named("product_swap", placed, product)
    panel_inverse = jnp.stack([-(in_pattern[n] * panels[n]) for n in range(CORES)])
    diags = named("diag_swap", placed, diag)
    diag_inverse = jnp.stack([child_base[n] - diags[n] for n in range(CORES)])
    return root_inverse, panel_inverse, diag_inverse


def pick_even(even, ours, theirs):
    return jnp.where(even, ours, theirs)


def solution(mesh):
    return jax.shard_map(
        shards,
        mesh=mesh,
        in_specs=(P("row", "col"), P("row"), P(), P(None, "col", "row"), P(None, "col", "row")),
        out_specs=(P("row", "col"), P(None, "col", "row"), P(None, "col", "row")),
        check_vma=False,
    )
```

```python
import jax
import jax.numpy as jnp
from jax import lax
from jax.sharding import PartitionSpec as P

BS = 256
SIDE = 4
CORES = 2
AXES = ("row", "col")


def place(index):
    row, col = divmod(index, SIDE * SIDE)
    return col % SIDE, col // SIDE, row // CORES, row % CORES


def number(x, y, z, core):
    return ((z % SIDE) * CORES + core) * SIDE * SIDE + (y % SIDE) * SIDE + x % SIDE


def move(value, target):
    total = SIDE * SIDE * SIDE * CORES
    pairs = [(index, number(*target(*place(index)))) for index in range(total)]
    return lax.ppermute(value, AXES, pairs)


def shift(value, axis, step):
    def target(x, y, z, core):
        if axis == "z":
            return x, y, z + step, core
        if axis == "x" or (axis == "along" and core == 0) or (axis == "across" and core == 1):
            return x + step, y, z, core
        return x, y + step, z, core

    return move(value, target)


def swap_cores(value):
    return move(value, lambda x, y, z, core: (x, y, z, 1 - core))


def gather(value, axis):
    return [value] + [shift(value, axis, -step) for step in (1, 2, 3)]


def scatter(pieces, axis):
    got = [shift(pieces[step], axis, step) for step in (1, 2, 3)]
    return pieces[0] + got[0] + got[1] + got[2]


def sides(value, axis):
    return shift(value, axis, -1), shift(value, axis, 1)


def opposite(above, below, axis):
    half = above.shape[0] // 2
    top, bottom = shift(below[:half], axis, 1), shift(above[half:], axis, -1)
    return jnp.concatenate([top, bottom], axis=0)


def relay(value):
    return move(value, lambda x, y, z, core: (x, y, z + 1 - 2 * core, core))


def after(value, *earlier):
    return lax.optimization_barrier((value,) + earlier)[0]


def named(name, call, *args):
    with jax.named_scope(name):
        return call(*args)


def dot(left, right, dims):
    return lax.dot_general(
        left,
        right,
        (dims, ((), ())),
        precision=lax.Precision.HIGH,
        preferred_element_type=jnp.float32,
    )


def tdot(left, right):
    return dot(left, right, ((0,), (0,)))


def ndot(left, right):
    return dot(left, right, ((1,), (0,)))


def take(value, at, size):
    return lax.dynamic_slice_in_dim(value, at * size, size, 0)


def shards(root_linv, root_pivinv, child_blocks, child_panel, child_base):
    row, col = lax.axis_index("row"), lax.axis_index("col")
    z, core = row // CORES, row % CORES
    y, x = col // SIDE, col % SIDE
    first, even = core == 0, x % 2 == 0
    steps = range(SIDE)
    wide = child_panel.shape[2]
    width = child_base.shape[1]

    def pick(ours, theirs):
        return jnp.where(first, ours, theirs)

    with jax.named_scope("root_rows"):
        above, below = sides(root_linv, "along")
        other = swap_cores(root_linv)
        above_other, below_other = sides(other, "along")
    with jax.named_scope("panel_planes"):
        lent = swap_cores(child_panel)
        near = relay(child_panel)
        passed = relay(after(lent, near, above_other))
    with jax.named_scope("root_rows"):
        far, far_other = shift(below, "along", 1), shift(above_other, "along", -1)
    with jax.named_scope("panel_planes"):
        far_other, passed = after((far_other, passed))
        beyond = relay(after(near, passed))
    rows = [root_linv, above, far, below], [other, above_other, far_other, below_other]

    with jax.named_scope("root_hand"):
        handed = [[kept[0]] + [swap_cores(value) for value in sent[1:]] for kept, sent in zip(rows, rows[::-1])]
        scales = root_pivinv, swap_cores(root_pivinv)

    terms = []
    for scale, kept, got in zip(scales, rows, handed):
        tall = jnp.concatenate([pick(got[step], kept[step]) for step in steps], axis=1)
        across = jnp.concatenate([pick(kept[step], got[step + 2]) for step in (0, 1)], axis=1)
        terms.append(tdot(scale[:, None] * tall, across))
    half = terms[0] + terms[1]

    def joined(low, high):
        return jnp.concatenate([low, high], axis=1)

    panel = joined(pick(child_panel[0], lent[1]), pick(lent[0], child_panel[1]))
    near_plane = joined(pick(near[0], passed[1]), pick(passed[0], near[1]))
    opposite_plane = joined(pick(near[1], passed[0]), pick(passed[1], near[0]))
    opposite_plane = named("panel_hand", swap_cores, opposite_plane)
    above_plane, below_plane = pick(opposite_plane, near_plane), pick(near_plane, opposite_plane)
    above, below = named("panel_rows", sides, after(panel, terms[0]), "across")
    half, panel, above_plane, below_plane = after((half, panel, above_plane, below_plane))

    got = named("panel_hand", swap_cores, pick(beyond[1], beyond[0]))
    above, below, got = after((above, below, got))
    slab = [panel, above, named("panel_rows", opposite, above, below, "across"), below]
    planes = [panel, above_plane, joined(pick(beyond[0], got), pick(got, beyond[1])), below_plane]
    stacked = jnp.concatenate(planes, axis=0)

    def columns(step):
        at = (x + step) % SIDE * width
        strips = [lax.dynamic_slice_in_dim(plane, at, width, 1) for plane in planes]
        return pick(jnp.concatenate(strips, axis=1), take(stacked, (y + step - z) % SIDE, BS))

    strips = [columns(step) for step in steps]

    with jax.named_scope("piece_sum"):
        pieces = [take(half, (z + step - y) % SIDE, BS) for step in steps]
        received = [shift(pieces[step], "z", step) for step in (1, 2, 3)]
        received, slab, strips = after((received, slab, strips))
        piece = pieces[0] + received[0] + received[1] + received[2]

    mine = named("block_gather", gather, piece, "z")
    with jax.named_scope("block_swap"):
        theirs = jnp.concatenate([swap_cores(value) for value in mine], axis=0)
    mine = jnp.concatenate(mine, axis=0)

    with jax.named_scope("panel_columns"):
        left = [shift(strips[3], "along", -1), shift(strips[1], "along", 1)]
        far = shift(after(strips[2], *left), "along", 2)
        left = jnp.concatenate([strips[0], left[0], far, left[1]], axis=0)

    slab = jnp.concatenate(slab, axis=0)
    slab = jnp.concatenate([take(slab, pick((z + step - y) % SIDE, step), BS) for step in steps], axis=0)

    def product_of_first(mine, theirs, slab):
        return jnp.concatenate([tdot(mine, slab), tdot(theirs, slab)], axis=0)

    def product_of_second(mine, theirs, slab):
        return ndot(mine, slab[2 * BS :]) + ndot(theirs, slab[: 2 * BS])

    part = lax.cond(first, product_of_first, product_of_second, mine, theirs, slab)
    part = after(part, far)
    part = [take(part, pick(step, (y + step - z) % SIDE), BS) for step in steps]
    product = named("product_sum", scatter, part, "along")

    gathered = named("product_rows", gather, product, "along")
    diag = tdot(left, jnp.concatenate(gathered, axis=0))

    turn = after(piece, diag)
    same = named("root_same", move, turn[:, :BS], lambda x, y, z, core: (x + 2 * core, y, z, x // 2))
    other = named("root_other", move, turn[:, BS:], lambda x, y, z, core: (x + 2 * core + 1, y, z, x // 2))

    diag = [take(diag, pick((y + step - z) % SIDE, (x + step) % SIDE), width) for step in steps]
    diag = named("diag_sum", scatter, diag, "across")
    diag, same, other = after((diag, same, other))

    root_inverse = jnp.concatenate([pick_even(even, same, other), pick_even(even, other, same)], axis=0)

    def placed(value):
        low, high = value[:, :wide], value[:, wide:]
        kept, got = pick(low, high), swap_cores(pick(high, low))
        return pick(kept, got), pick(got, kept)

    in_pattern = jnp.any(child_blocks == col, axis=1).astype(jnp.float32)
    panels = named("product_swap", placed, product)
    panel_inverse = jnp.stack([-(in_pattern[n] * panels[n]) for n in range(CORES)])
    diags = named("diag_swap", placed, diag)
    diag_inverse = jnp.stack([child_base[n] - diags[n] for n in range(CORES)])
    return root_inverse, panel_inverse, diag_inverse


def pick_even(even, ours, theirs):
    return jnp.where(even, ours, theirs)


def solution(mesh):
    return jax.shard_map(
        shards,
        mesh=mesh,
        in_specs=(P("row", "col"), P("row"), P(), P(None, "col", "row"), P(None, "col", "row")),
        out_specs=(P("row", "col"), P(None, "col", "row"), P(None, "col", "row")),
        check_vma=False,
    )
```

```python
import jax
import jax.numpy as jnp
from jax import lax
from jax.sharding import PartitionSpec as P

BS = 256
SIDE = 4
CORES = 2
AXES = ("row", "col")


def place(index):
    row, col = divmod(index, SIDE * SIDE)
    return col % SIDE, col // SIDE, row // CORES, row % CORES


def number(x, y, z, core):
    return ((z % SIDE) * CORES + core) * SIDE * SIDE + (y % SIDE) * SIDE + x % SIDE


def move(value, target):
    total = SIDE * SIDE * SIDE * CORES
    pairs = [(index, number(*target(*place(index)))) for index in range(total)]
    return lax.ppermute(value, AXES, pairs)


def shift(value, axis, step):
    def target(x, y, z, core):
        if axis == "z":
            return x, y, z + step, core
        if axis == "x" or (axis == "along" and core == 0) or (axis == "across" and core == 1):
            return x + step, y, z, core
        return x, y + step, z, core

    return move(value, target)


def swap_cores(value):
    return move(value, lambda x, y, z, core: (x, y, z, 1 - core))


def gather(value, axis):
    return [value] + [shift(value, axis, -step) for step in (1, 2, 3)]


def scatter(pieces, axis):
    got = [shift(pieces[step], axis, step) for step in (1, 2, 3)]
    return pieces[0] + got[0] + got[1] + got[2]


def sides(value, axis):
    return shift(value, axis, -1), shift(value, axis, 1)


def opposite(above, below, axis):
    half = above.shape[0] // 2
    top, bottom = shift(below[:half], axis, 1), shift(above[half:], axis, -1)
    return jnp.concatenate([top, bottom], axis=0)


def relay(value):
    return move(value, lambda x, y, z, core: (x, y, z + 1 - 2 * core, core))


def after(value, *earlier):
    return lax.optimization_barrier((value,) + earlier)[0]


def named(name, call, *args):
    with jax.named_scope(name):
        return call(*args)


def dot(left, right, dims):
    return lax.dot_general(
        left,
        right,
        (dims, ((), ())),
        precision=lax.Precision.HIGH,
        preferred_element_type=jnp.float32,
    )


def tdot(left, right):
    return dot(left, right, ((0,), (0,)))


def ndot(left, right):
    return dot(left, right, ((1,), (0,)))


def take(value, at, size):
    return lax.dynamic_slice_in_dim(value, at * size, size, 0)


def shards(root_linv, root_pivinv, child_blocks, child_panel, child_base):
    row, col = lax.axis_index("row"), lax.axis_index("col")
    z, core = row // CORES, row % CORES
    y, x = col // SIDE, col % SIDE
    first, even = core == 0, x % 2 == 0
    steps = range(SIDE)
    wide = child_panel.shape[2]
    width = child_base.shape[1]

    def pick(ours, theirs):
        return jnp.where(first, ours, theirs)

    with jax.named_scope("root_rows"):
        above, below = sides(root_linv, "along")
        other = swap_cores(root_linv)
        above_other, below_other = sides(other, "along")
    with jax.named_scope("panel_planes"):
        lent = swap_cores(child_panel)
        near = relay(child_panel)
        passed = relay(after(lent, near, above_other))
    with jax.named_scope("root_rows"):
        far, far_other = shift(below, "along", 1), shift(above_other, "along", -1)
    with jax.named_scope("panel_planes"):
        far_other, passed = after((far_other, passed))
        beyond = relay(after(near, passed))
    rows = [root_linv, above, far, below], [other, above_other, far_other, below_other]

    with jax.named_scope("root_hand"):
        handed = [[kept[0]] + [swap_cores(value) for value in sent[1:]] for kept, sent in zip(rows, rows[::-1])]
        scales = root_pivinv, swap_cores(root_pivinv)

    terms = []
    for scale, kept, got in zip(scales, rows, handed):
        tall = jnp.concatenate([pick(got[step], kept[step]) for step in steps], axis=1)
        across = jnp.concatenate([pick(kept[step], got[step + 2]) for step in (0, 1)], axis=1)
        terms.append(tdot(scale[:, None] * tall, across))
    half = terms[0] + terms[1]

    def joined(low, high):
        return jnp.concatenate([low, high], axis=1)

    panel = joined(pick(child_panel[0], lent[1]), pick(lent[0], child_panel[1]))
    near_plane = joined(pick(near[0], passed[1]), pick(passed[0], near[1]))
    opposite_plane = joined(pick(near[1], passed[0]), pick(passed[1], near[0]))
    opposite_plane = named("panel_hand", swap_cores, opposite_plane)
    above_plane, below_plane = pick(opposite_plane, near_plane), pick(near_plane, opposite_plane)
    above, below = named("panel_rows", sides, after(panel, terms[0]), "across")
    half, panel, above_plane, below_plane = after((half, panel, above_plane, below_plane))

    got = named("panel_hand", swap_cores, pick(beyond[1], beyond[0]))
    above, below, got = after((above, below, got))
    slab = [panel, above, named("panel_rows", opposite, above, below, "across"), below]
    planes = [panel, above_plane, joined(pick(beyond[0], got), pick(got, beyond[1])), below_plane]
    stacked = jnp.concatenate(planes, axis=0)

    def columns(step):
        at = (x + step) % SIDE * width
        strips = [lax.dynamic_slice_in_dim(plane, at, width, 1) for plane in planes]
        return pick(jnp.concatenate(strips, axis=1), take(stacked, (y + step - z) % SIDE, BS))

    strips = [columns(step) for step in steps]

    with jax.named_scope("piece_sum"):
        pieces = [take(half, (z + step - y) % SIDE, BS) for step in steps]
        received = [shift(pieces[step], "z", step) for step in (1, 2, 3)]
        received, slab, strips = after((received, slab, strips))
        piece = pieces[0] + received[0] + received[1] + received[2]

    mine = named("block_gather", gather, piece, "z")
    with jax.named_scope("block_swap"):
        theirs = jnp.concatenate([swap_cores(value) for value in mine], axis=0)
    mine = jnp.concatenate(mine, axis=0)

    with jax.named_scope("panel_columns"):
        left = [shift(strips[3], "along", -1), shift(strips[1], "along", 1)]
        far = shift(after(strips[2], *left), "along", 2)
        left = jnp.concatenate([strips[0], left[0], far, left[1]], axis=0)

    slab = jnp.concatenate(slab, axis=0)
    slab = jnp.concatenate([take(slab, pick((z + step - y) % SIDE, step), BS) for step in steps], axis=0)

    def product_of_first(mine, theirs, slab):
        parts = tdot(mine, slab), tdot(theirs, slab)
        return [part[at : at + BS] for part in parts for at in (0, BS)]

    def product_of_second(mine, theirs, slab):
        part = ndot(mine, slab[2 * BS :]) + ndot(theirs, slab[: 2 * BS])
        return [take(part, (y + step - z) % SIDE, BS) for step in steps]

    part = lax.cond(first, product_of_first, product_of_second, mine, theirs, slab)
    part = after(part, far)
    product = named("product_sum", scatter, part, "along")

    gathered = named("product_rows", gather, product, "along")
    diag = tdot(left, jnp.concatenate(gathered, axis=0))

    turn = after(piece, diag)
    same = named("root_same", move, turn[:, :BS], lambda x, y, z, core: (x + 2 * core, y, z, x // 2))
    other = named("root_other", move, turn[:, BS:], lambda x, y, z, core: (x + 2 * core + 1, y, z, x // 2))

    diag = [take(diag, pick((y + step - z) % SIDE, (x + step) % SIDE), width) for step in steps]
    diag = named("diag_sum", scatter, diag, "across")
    diag, same, other = after((diag, same, other))

    root_inverse = jnp.concatenate([pick_even(even, same, other), pick_even(even, other, same)], axis=0)

    def placed(value):
        low, high = value[:, :wide], value[:, wide:]
        kept, got = pick(low, high), swap_cores(pick(high, low))
        return pick(kept, got), pick(got, kept)

    in_pattern = jnp.any(child_blocks == col, axis=1).astype(jnp.float32)
    panels = named("product_swap", placed, product)
    panel_inverse = jnp.stack([-(in_pattern[n] * panels[n]) for n in range(CORES)])
    diags = named("diag_swap", placed, diag)
    diag_inverse = jnp.stack([child_base[n] - diags[n] for n in range(CORES)])
    return root_inverse, panel_inverse, diag_inverse


def pick_even(even, ours, theirs):
    return jnp.where(even, ours, theirs)


def solution(mesh):
    return jax.shard_map(
        shards,
        mesh=mesh,
        in_specs=(P("row", "col"), P("row"), P(), P(None, "col", "row"), P(None, "col", "row")),
        out_specs=(P("row", "col"), P(None, "col", "row"), P(None, "col", "row")),
        check_vma=False,
    )
```
